512 devices in a mesh: wide: 32 (over y_lo, z), tp: 16 (over y_hi, x, core).
Axes of the slice: x: 4, y: 8 (y_hi: 2, y_lo: 4; y = y_hi * 4 + y_lo), z: 8, core: 2. Of those that a mesh axis runs over, the one named last changes fastest.
Arguments:
- hidden_in: bfloat16 [64, 16384], P(None, 'wide'), may hold values from -6 to 6
- q_weight: bfloat16 [16384, 16384], P('wide', 'tp'), may hold values from -0.046875 to 0.046875
- kv_weight: bfloat16 [16384, 2048], P('wide', 'tp'), may hold values from -0.046875 to 0.046875
- o_weight: bfloat16 [16384, 16384], P('tp', 'wide'), may hold values from -0.046875 to 0.046875
- cache_keys: bfloat16 [64, 1024, 1024], P('tp', 'wide'), may hold values from -1000 to 1000, as said below
- cache_values: bfloat16 [64, 1024, 1024], P('tp', 'wide'), may hold values from -6 to 6
- lengths: int32 [64], P('tp'), may hold values from 1 to 1024, as said below
- positions: int32 [64], P('tp'), may hold values from 0 to 8191
Outputs:
- attended: bfloat16 [64, 16384], P('tp', 'wide')
- new_kv: bfloat16 [64, 2048], P('tp')
The draws below stay inside these ranges and needn't reach their ends.
Inputs may be any that keep to these rules, and one draw needn't show every extreme that they name: `cache_keys`: keys already carry the rotary embedding of their positions. Row b's cache holds valid entries in its first lengths[b] rows; some row fills all 1024.
All inputs are finite; a program needn't handle non-finite values.
Results may differ from the reference program's by a relative error of at most 0.015.
The reference program's roundings to bfloat16 on the way count: a program that leaves them out, or rounds other values in their place, can miss the bound.
Values may be sent and summed in bfloat16 or wider, within the bound.
No kernel may reach another device: no remote copies, remote signals or barrier semaphores. Data moves between devices by JAX's collectives and lax.ppermute only.
A program may use at most 64 MiB of HBM per device.

```python
import math
import jax
import jax.numpy as jnp
from jax import lax

D = 16384
NH = 128
KVH = 8
DH = 128
B = 64
CTX = 1024


def draw_cache_keys(key, part):
    key = jax.random.fold_in(key, 11)
    first_key, second_key = jax.random.split(key, 2)
    scale = jnp.exp(jax.random.uniform(first_key, (B, CTX, 1), jnp.float32, math.log(0.5), math.log(2.0)))
    base = jax.random.normal(second_key, (B, CTX, KVH * DH), jnp.float32) * scale
    return base.astype(jnp.bfloat16)


def draw_lengths(key, part):
    key = jax.random.fold_in(key, 5)
    first_key, second_key = jax.random.split(key)
    filled = jax.random.randint(first_key, (B,), 1, CTX + 1)
    chosen = jax.random.randint(second_key, (), 0, B)
    return jnp.where(jnp.arange(B, dtype=jnp.int32) == chosen, CTX, filled).astype(jnp.int32)


def set_ends(result, rng, smallest, top_value):
    place = [jax.random.randint(jax.random.fold_in(rng, axis), (), 0, length) for axis, length in enumerate(result.shape)]
    longest = result.shape.index(max(result.shape))
    next_to = place[:longest] + [(place[longest] + 1) % result.shape[longest]] + place[longest + 1:]
    return result.at[tuple(place)].set(smallest).at[tuple(next_to)].set(top_value)


def level_of(key, extent, pieces, low, largest):
    def one(dim, shards_of):
        heights = jax.random.uniform(jax.random.fold_in(jax.random.fold_in(key, 6), dim), (shards_of,), jnp.float32, low / len(pieces), largest / len(pieces))
        return jnp.repeat(jnp.exp(heights), extent[dim] // shards_of).reshape((-1,) + (1,) * (len(extent) - dim - 1))

    loudness = one(*pieces[0])
    for cut in pieces[1:]:
        loudness = loudness * one(*cut)
    return loudness


def centred(rng, shape, scale, reach, cuts=(), kind=jnp.bfloat16):
    values = scale * jax.random.normal(rng, shape, jnp.float32)
    if cuts:
        values = values * level_of(rng, shape, cuts, -0.22, 0.18)
    return jnp.clip(values, -reach, reach).astype(kind)


def setup_inputs(seed: int = 0) -> dict:
    streams_of = jax.random.split(jax.random.key(seed), 9)
    return {
        "hidden_in": centred(streams_of[0], (B, D), 1.0, 6.0, ((1, 32),)),
        "q_weight": centred(streams_of[1], (D, NH * DH), D ** -0.5, 0.046875, ((0, 32), (1, 16))),
        "kv_weight": centred(streams_of[2], (D, 2 * KVH * DH), D ** -0.5, 0.046875, ((0, 32), (1, 16))),
        "o_weight": centred(streams_of[3], (NH * DH, D), (NH * DH) ** -0.5, 0.046875, ((0, 16), (1, 32))),
        "cache_keys": draw_cache_keys(jax.random.fold_in(streams_of[8], 71), 0),
        "cache_values": centred(streams_of[5], (B, CTX, KVH * DH), 1.0, 6.0, ((0, 16), (1, 32))),
        "lengths": draw_lengths(jax.random.fold_in(streams_of[8], 71), 0),
        "positions": set_ends(jax.random.randint(streams_of[7], (B,), 0, 8192), jax.random.fold_in(streams_of[7], 1), 0, 8191).astype(jnp.int32),
    }


LOWEST = -1e30


def rotate(block, positions):
    half = block.shape[-1] // 2
    freq = 500000.0 ** (-(jnp.arange(half, dtype=jnp.float32) * 2.0 / block.shape[-1]))
    angle = positions.astype(jnp.float32)[:, None] * freq[None, :]
    cosine = jnp.cos(angle)[:, None, :]
    sine = jnp.sin(angle)[:, None, :]
    first = block[..., :half]
    second = block[..., half:]
    return jnp.concatenate([first * cosine - second * sine, second * cosine + first * sine], -1)


def reference(hidden_in, q_weight, kv_weight, o_weight, cache_keys, cache_values, lengths, positions):
    batch = hidden_in.shape[0]
    groups = NH // KVH
    factor = DH ** -0.5
    query_raw = jnp.dot(hidden_in, q_weight, preferred_element_type=jnp.float32).astype(jnp.bfloat16)
    fresh = jnp.dot(hidden_in, kv_weight, preferred_element_type=jnp.float32).astype(jnp.bfloat16)
    query = rotate(query_raw.astype(jnp.float32).reshape(batch, NH, DH), positions).astype(jnp.bfloat16)
    new_keys = rotate(fresh[:, :KVH * DH].astype(jnp.float32).reshape(batch, KVH, DH), positions).astype(jnp.bfloat16)
    new_values = fresh[:, KVH * DH:].reshape(batch, KVH, DH)
    new_kv = jnp.concatenate([new_keys.reshape(batch, KVH * DH), fresh[:, KVH * DH:]], 1)

    def attend(item):
        one_query, keys, values, length, own_key, own_value = item
        query_f = one_query.astype(jnp.float32).reshape(KVH, groups, DH)
        keys_f = keys.astype(jnp.float32).reshape(CTX, KVH, DH)
        values_f = values.astype(jnp.float32).reshape(CTX, KVH, DH)
        scores = jnp.einsum("kgd,ckd->kgc", query_f, keys_f) * factor
        own = jnp.einsum("kgd,kd->kg", query_f, own_key.astype(jnp.float32)) * factor
        valid = jnp.arange(CTX, dtype=jnp.int32) < length
        top = jnp.maximum(jnp.max(jnp.where(valid, scores, LOWEST), -1), own)
        weight = jnp.where(valid, jnp.exp(scores - top[..., None]), 0.0)
        weight_own = jnp.exp(own - top)
        total = jnp.sum(weight, -1) + weight_own
        weight_b = lax.optimization_barrier(weight.astype(jnp.bfloat16))
        own_b = lax.optimization_barrier(weight_own.astype(jnp.bfloat16))
        mixed = jnp.einsum("kgc,ckd->kgd", weight_b.astype(jnp.float32), values_f)
        mixed = mixed + own_b.astype(jnp.float32)[..., None] * own_value.astype(jnp.float32)[:, None, :]
        return (mixed / total[..., None]).astype(jnp.bfloat16).reshape(NH * DH)

    attention = lax.map(attend, (query, cache_keys, cache_values, lengths, new_keys, new_values))
    attended = jnp.dot(attention, o_weight, preferred_element_type=jnp.float32).astype(jnp.bfloat16)
    return attended, new_kv
```

```python
import jax
import jax.numpy as jnp
from jax import lax
from jax.sharding import Mesh
from jax.sharding import PartitionSpec as P

NH = 128
KVH = 8
DH = 128
GROUP = NH // KVH

LOWEST = -1e30

AXES = ("yl", "z", "yh", "x", "core")
SIZES = (4, 8, 2, 4, 2)
WIDE = ("yl", "z")
TP = ("yh", "x", "core")
ROWS = ("yl", "yh", "x", "core")


def exchange(array, axes):
    return lax.all_to_all(array, axes, split_axis=0, concat_axis=0, tiled=True)


def rotate(block, position):
    half = block.shape[-1] // 2
    freq = 500000.0 ** (-(jnp.arange(half, dtype=jnp.float32) * 2.0 / block.shape[-1]))
    angle = position.astype(jnp.float32) * freq
    cosine = jnp.cos(angle)
    sine = jnp.sin(angle)
    first = block[..., :half]
    second = block[..., half:]
    return jnp.concatenate([first * cosine - second * sine, second * cosine + first * sine], -1)


def per_device(
    hidden_in, q_weight, kv_weight, o_weight, cache_keys, cache_values, lengths, positions
):
    f32, bf16 = jnp.float32, jnp.bfloat16
    seqs, span = cache_keys.shape[:2]
    tp = 16

    partial = jnp.concatenate(
        [
            jnp.dot(hidden_in, q_weight, preferred_element_type=f32).astype(bf16),
            jnp.dot(hidden_in, kv_weight, preferred_element_type=f32).astype(bf16),
        ],
        1,
    ).reshape(tp, seqs, -1)
    partial = exchange(partial, TP)

    q_part = partial[:, :, : GROUP * DH // 2].reshape(KVH, 2, seqs, GROUP // 2, DH)
    q_part = q_part.transpose(2, 0, 1, 3, 4).reshape(seqs, KVH, GROUP, DH)
    kv_part = partial[:, :, GROUP * DH // 2 :].reshape(2, KVH, seqs, DH).transpose(2, 1, 0, 3)
    keys = cache_keys.reshape(seqs, span, KVH, DH).transpose(0, 2, 1, 3)
    values = cache_values.reshape(seqs, span, KVH, DH).transpose(0, 2, 1, 3)
    blank = jnp.zeros((seqs, KVH, 6, DH), bf16)
    packed = jnp.concatenate([keys, values, q_part, kv_part, blank], 2)
    packed = exchange(packed.reshape(seqs * KVH, -1, DH), WIDE)

    keys = packed[:, :span].reshape(-1, DH)
    values = packed[:, span : 2 * span].reshape(-1, DH)
    sums = jnp.sum(packed[:, 2 * span :].astype(f32), 0).astype(bf16)
    mine = lax.axis_index("yl")
    length = lengths[mine]
    position = positions[mine]
    turned = rotate(sums[: GROUP + 1].astype(f32), position).astype(bf16)
    query = turned[:GROUP]
    new_key = turned[GROUP]
    new_value = sums[GROUP + 1]

    factor = DH ** (-0.5)
    scores = jnp.dot(query, keys.T, preferred_element_type=f32) * factor
    own = jnp.dot(query, new_key, preferred_element_type=f32) * factor
    valid = (jnp.arange(keys.shape[0], dtype=jnp.int32) < length)[None, :]
    top = jnp.maximum(jnp.max(jnp.where(valid, scores, LOWEST), -1), own)
    weight = jnp.where(valid, jnp.exp(scores - top[:, None]), 0.0)
    weight_own = jnp.exp(own - top)
    total = jnp.sum(weight, -1) + weight_own
    mixed = jnp.dot(weight.astype(bf16), values, preferred_element_type=f32)
    mixed = mixed + weight_own.astype(bf16).astype(f32)[:, None] * new_value.astype(f32)[None, :]
    attention = (mixed / total[:, None]).astype(bf16)

    row = jnp.concatenate([attention, new_key[None], new_value[None], jnp.zeros((6, DH), bf16)], 0)
    heads = exchange(jnp.broadcast_to(row[None], (KVH,) + row.shape), ("z",))
    piece = jnp.concatenate(
        [
            heads[:, :GROUP].reshape(tp, GROUP // 2, DH),
            heads[:, GROUP : GROUP + 2].transpose(1, 0, 2).reshape(tp, 1, DH),
        ],
        1,
    )
    piece = jnp.broadcast_to(piece[None], (seqs,) + piece.shape).reshape(seqs * tp, -1, DH)
    piece = exchange(piece, ROWS)
    flat = piece[:, : GROUP // 2].reshape(seqs * tp, -1)
    product = jnp.dot(flat, o_weight, preferred_element_type=f32).astype(bf16)
    out = jnp.concatenate([product, piece[:, GROUP // 2]], 1)
    out = out.reshape(seqs, tp, -1).transpose(1, 0, 2)
    out = exchange(out, TP)
    width = o_weight.shape[1]
    attended = jnp.sum(out[:, :, :width].astype(f32), 0).astype(bf16)
    new_kv = out[:, :, width:].transpose(1, 0, 2).reshape(seqs, -1)
    return (attended, new_kv)


def solution(mesh):
    fine = Mesh(mesh.devices.reshape(SIZES), AXES)
    in_specs = (
        P(None, WIDE),
        P(WIDE, TP),
        P(WIDE, TP),
        P(TP, WIDE),
        P(TP, WIDE, None),
        P(TP, WIDE, None),
        P(TP),
        P(TP),
    )
    out_specs = (P(TP, WIDE), P(TP, None))
    return jax.shard_map(
        per_device, mesh=fine, in_specs=in_specs, out_specs=out_specs, check_vma=False
    )
```

```python
import functools

import jax
import jax.numpy as jnp
import numpy as np
from jax import lax
from jax.experimental import pallas as pl
from jax.experimental.pallas import tpu as pltpu
from jax.sharding import Mesh
from jax.sharding import PartitionSpec as P

NH = 128
KVH = 8
DH = 128
GROUP = NH // KVH
HALF = GROUP // 2

LOWEST = -1e30
LIMIT = 8 * 2**20

AXES = ("yl", "z", "yh", "x", "core")
SIZES = (4, 8, 2, 4, 2)
WIDE = ("yl", "z")
TP = ("yh", "x", "core")


def exchange(array, axes):
    return lax.all_to_all(array, axes, split_axis=0, concat_axis=0, tiled=True)


def frequencies():
    half = DH // 2
    power = -(np.arange(half, dtype=np.float32) * np.float32(2.0) / np.float32(DH))
    freq = np.power(np.float64(500000.0), power.astype(np.float64)).astype(np.float32)
    return np.concatenate([freq, freq])[None]


def call(kernel, out_shape, in_specs, name, **options):
    return pl.pallas_call(
        kernel,
        out_shape=out_shape,
        in_specs=in_specs,
        out_specs=jax.tree.map(lambda _: pl.BlockSpec(memory_space=pltpu.VMEM), out_shape),
        compiler_params=pltpu.CompilerParams(vmem_limit_bytes=LIMIT),
        name=name,
        **options,
    )


IN_VMEM = pl.BlockSpec(memory_space=pltpu.VMEM)


def prepare_kernel(
    keys_ref, values_ref, freq_ref, lengths_ref, positions_ref, packed_ref, turn_ref, valid_ref
):
    seqs, span = keys_ref.shape[:2]
    pairs = span // 2
    for seq in range(seqs):
        for head in range(KVH):
            place = seq * KVH + head
            columns = pl.ds(head * DH, DH)
            packed_ref[place, :pairs] = keys_ref[seq, :, columns].reshape(pairs, 2, DH)
            packed_ref[place, pairs : 2 * pairs] = values_ref[seq, :, columns].reshape(pairs, 2, DH)
    lane = lax.broadcasted_iota(jnp.int32, lengths_ref.shape, 1)
    chosen = lane == lax.axis_index("yl")
    length = jnp.sum(jnp.where(chosen, lengths_ref[...], 0), axis=1, keepdims=True)
    position = jnp.sum(jnp.where(chosen, positions_ref[...], 0), axis=1, keepdims=True)
    valid = lax.broadcasted_iota(jnp.int32, valid_ref.shape, 1) < length
    valid_ref[...] = valid.astype(jnp.float32)
    angle = position.astype(jnp.float32) * freq_ref[...]
    sine = jnp.sin(angle)
    first_half = lax.broadcasted_iota(jnp.int32, sine.shape, 1) < DH // 2
    turn_ref[0:1] = jnp.cos(angle)
    turn_ref[1:2] = jnp.where(first_half, -sine, sine)


def prepare(cache_keys, cache_values, freq, lengths, positions, rows, places):
    seqs = cache_keys.shape[0]
    return call(
        prepare_kernel,
        [
            jax.ShapeDtypeStruct((seqs * KVH, rows // 2, 2, DH), cache_keys.dtype),
            jax.ShapeDtypeStruct((2, DH), jnp.float32),
            jax.ShapeDtypeStruct((1, places), jnp.float32),
        ],
        [IN_VMEM] * 5,
        "prepare",
    )(cache_keys, cache_values, freq, lengths[None], positions[None])


def place_kernel(packed_ref, fresh_ref, out_ref):
    del packed_ref
    count, rows = fresh_ref.shape[:2]
    fresh = fresh_ref[...].reshape(count, rows // 2, 2, DH)
    out_ref[:, out_ref.shape[1] - rows // 2 :] = fresh


def place(packed, fresh):
    return call(
        place_kernel,
        jax.ShapeDtypeStruct(packed.shape, packed.dtype),
        [IN_VMEM] * 2,
        "place",
        input_output_aliases={0: 0},
    )(packed, fresh)


def attention_kernel(packed_ref, turn_ref, valid_ref, out_ref, *, span):
    f32, bf16 = jnp.float32, jnp.bfloat16
    sources = packed_ref.shape[0]
    pairs = span // 2
    sums = packed_ref[0, 2 * pairs :].reshape(-1, DH).astype(f32)
    for source in range(1, sources):
        sums = sums + packed_ref[source, 2 * pairs :].reshape(-1, DH).astype(f32)
    sums = sums.astype(bf16)
    plain = sums.astype(f32)
    swapped = pltpu.roll(plain, DH // 2, 1)
    turned = (plain * turn_ref[0:1] + swapped * turn_ref[1:2]).astype(bf16)
    query = turned[:GROUP]
    new_key = turned[GROUP : GROUP + 1]
    new_value = sums[GROUP + 1 : GROUP + 2]

    factor = DH ** (-0.5)
    keys = packed_ref[:, :pairs].reshape(-1, DH)
    values = packed_ref[:, pairs : 2 * pairs].reshape(-1, DH)
    scores = lax.dot_general(
        query, keys, (((1,), (1,)), ((), ())), preferred_element_type=f32
    ) * factor
    own = jnp.sum(query.astype(f32) * new_key.astype(f32), -1, keepdims=True) * factor
    valid = valid_ref[...] > 0
    top = jnp.maximum(jnp.max(jnp.where(valid, scores, LOWEST), -1, keepdims=True), own)
    weight = jnp.where(valid, jnp.exp(scores - top), 0.0)
    weight_own = jnp.exp(own - top)
    total = jnp.sum(weight, -1, keepdims=True) + weight_own
    mixed = jnp.dot(weight.astype(bf16), values, preferred_element_type=f32)
    mixed = mixed + weight_own.astype(bf16).astype(f32) * new_value.astype(f32)
    attention = (mixed / total).astype(bf16)

    for half, extra in enumerate((new_key, new_value)):
        first = half * HALF
        rows = jnp.concatenate([attention[first : first + HALF], extra, extra], 0)
        out_ref[:, half] = jnp.broadcast_to(rows[None], (out_ref.shape[0],) + rows.shape)


def attend(packed, turn, valid, span):
    return call(
        functools.partial(attention_kernel, span=span),
        jax.ShapeDtypeStruct((KVH, 2, HALF + 2, DH), jnp.bfloat16),
        [IN_VMEM] * 3,
        "attend",
    )(packed, turn, valid)


def finish_kernel(parts_ref, attended_ref, new_kv_ref):
    width = attended_ref.shape[1]
    sources = parts_ref.shape[0]
    sums = parts_ref[0, :, :width].astype(jnp.float32)
    for source in range(1, sources):
        sums = sums + parts_ref[source, :, :width].astype(jnp.float32)
    attended_ref[...] = sums.astype(attended_ref.dtype)
    for source in range(sources):
        column = (source % 2 * KVH + source // 2) * DH
        new_kv_ref[:, pl.ds(column, DH)] = parts_ref[source, :, width:]


def finish(parts, width):
    sources, seqs = parts.shape[:2]
    return call(
        finish_kernel,
        [
            jax.ShapeDtypeStruct((seqs, width), parts.dtype),
            jax.ShapeDtypeStruct((seqs, sources * DH), parts.dtype),
        ],
        [IN_VMEM],
        "finish",
    )(parts)


def per_device(
    hidden_in, q_weight, kv_weight, o_weight, cache_keys, cache_values, lengths, positions
):
    f32, bf16 = jnp.float32, jnp.bfloat16
    seqs, span = cache_keys.shape[:2]
    tp = lax.axis_size(TP)
    batch = hidden_in.shape[0]
    rows = 2 * span + GROUP + 2
    places = span * lax.axis_size(WIDE)

    packed, turn, valid = prepare(
        cache_keys, cache_values, frequencies(), lengths, positions, rows, places
    )
    q_part = jnp.dot(hidden_in, q_weight, preferred_element_type=f32).astype(bf16)
    kv_part = jnp.dot(hidden_in, kv_weight, preferred_element_type=f32).astype(bf16)
    partial = jnp.concatenate([q_part, kv_part], 1).reshape(tp, seqs, -1)
    partial, packed, turn, valid = lax.optimization_barrier((partial, packed, turn, valid))
    partial = exchange(partial, TP)

    q_rows = partial[:, :, : HALF * DH].reshape(KVH, 2, seqs, HALF, DH)
    q_rows = q_rows.transpose(2, 0, 1, 3, 4).reshape(seqs, KVH, GROUP, DH)
    kv_rows = partial[:, :, HALF * DH :].reshape(2, KVH, seqs, DH).transpose(2, 1, 0, 3)
    fresh = jnp.concatenate([q_rows, kv_rows], 2)
    packed = place(packed, fresh.reshape(seqs * KVH, -1, DH))
    packed = exchange(packed, WIDE)
    heads = attend(packed, turn, valid, span)

    heads = exchange(heads.reshape((KVH * 2,) + heads.shape[2:]), ("z", "core"))
    middle = HALF * DH // 2
    mixed = heads[:, :HALF].reshape(KVH, 2, 2, middle)
    fresh = heads[:, HALF : HALF + 2].reshape(KVH, 2, 2, DH)
    piece = jnp.concatenate([mixed, fresh], 3)
    piece = jnp.broadcast_to(piece[:, None], (KVH, seqs) + piece.shape[1:])
    piece = exchange(piece.reshape((KVH * seqs,) + piece.shape[2:]), ("yh", "x", "yl"))
    flat = jnp.concatenate([piece[:, :, 0, :middle], piece[:, :, 1, :middle]], 2)
    product = jnp.dot(flat.reshape(batch, -1), o_weight, preferred_element_type=f32).astype(bf16)
    out = jnp.concatenate([product, piece[:, :, 0, middle:].reshape(batch, -1)], 1)
    out = out.reshape(KVH, seqs, 2, -1).transpose(0, 2, 1, 3).reshape(tp, seqs, -1)
    out = exchange(out, TP)
    return finish(out, o_weight.shape[1])


def solution(mesh):
    fine = Mesh(mesh.devices.reshape(SIZES), AXES)
    in_specs = (
        P(None, WIDE),
        P(WIDE, TP),
        P(WIDE, TP),
        P(TP, WIDE),
        P(TP, WIDE, None),
        P(TP, WIDE, None),
        P(TP),
        P(TP),
    )
    out_specs = (P(TP, WIDE), P(TP, None))
    return jax.shard_map(
        per_device, mesh=fine, in_specs=in_specs, out_specs=out_specs, check_vma=False
    )
```

```python
import functools

import jax
import jax.numpy as jnp
import numpy as np
from jax import lax
from jax.experimental import pallas as pl
from jax.experimental.pallas import tpu as pltpu
from jax.sharding import Mesh
from jax.sharding import PartitionSpec as P

NH = 128
KVH = 8
DH = 128
GROUP = NH // KVH
HALF = GROUP // 2

LOWEST = -1e30
LIMIT = 8 * 2**20

AXES = ("yl", "z", "yh", "x", "core")
SIZES = (4, 8, 2, 4, 2)
WIDE = ("yl", "z")
TP = ("yh", "x", "core")


def exchange(array, axes):
    return lax.all_to_all(array, axes, split_axis=0, concat_axis=0, tiled=True)


def frequencies():
    half = DH // 2
    power = -(np.arange(half, dtype=np.float32) * np.float32(2.0) / np.float32(DH))
    freq = np.power(np.float64(500000.0), power.astype(np.float64)).astype(np.float32)
    return np.concatenate([freq, freq])[None]


def call(kernel, out_shape, in_specs, name, **options):
    return pl.pallas_call(
        kernel,
        out_shape=out_shape,
        in_specs=in_specs,
        out_specs=jax.tree.map(lambda _: pl.BlockSpec(memory_space=pltpu.VMEM), out_shape),
        compiler_params=pltpu.CompilerParams(vmem_limit_bytes=LIMIT),
        name=name,
        **options,
    )


IN_VMEM = pl.BlockSpec(memory_space=pltpu.VMEM)


def prepare_kernel(
    keys_ref, values_ref, freq_ref, lengths_ref, positions_ref, packed_ref, turn_ref, valid_ref
):
    seqs, span = keys_ref.shape[:2]
    pairs = span // 2
    for seq in range(seqs):
        for head in range(KVH):
            place = seq * KVH + head
            columns = pl.ds(head * DH, DH)
            packed_ref[place, :pairs] = keys_ref[seq, :, columns].reshape(pairs, 2, DH)
            packed_ref[place, pairs : 2 * pairs] = values_ref[seq, :, columns].reshape(pairs, 2, DH)
    lane = lax.broadcasted_iota(jnp.int32, lengths_ref.shape, 1)
    chosen = lane == lax.axis_index("yl")
    length = jnp.sum(jnp.where(chosen, lengths_ref[...], 0), axis=1, keepdims=True)
    position = jnp.sum(jnp.where(chosen, positions_ref[...], 0), axis=1, keepdims=True)
    valid = lax.broadcasted_iota(jnp.int32, valid_ref.shape, 1) < length
    valid_ref[...] = valid.astype(jnp.float32)
    angle = position.astype(jnp.float32) * freq_ref[...]
    sine = jnp.sin(angle)
    first_half = lax.broadcasted_iota(jnp.int32, sine.shape, 1) < DH // 2
    turn_ref[0:1] = jnp.cos(angle)
    turn_ref[1:2] = jnp.where(first_half, -sine, sine)


def prepare(cache_keys, cache_values, freq, lengths, positions, rows, places):
    seqs = cache_keys.shape[0]
    return call(
        prepare_kernel,
        [
            jax.ShapeDtypeStruct((seqs * KVH, rows // 2, 2, DH), cache_keys.dtype),
            jax.ShapeDtypeStruct((2, DH), jnp.float32),
            jax.ShapeDtypeStruct((1, places), jnp.float32),
        ],
        [IN_VMEM] * 5,
        "prepare",
    )(cache_keys, cache_values, freq, lengths[None], positions[None])


def place_kernel(packed_ref, fresh_ref, out_ref):
    del packed_ref
    count, rows = fresh_ref.shape[:2]
    fresh = fresh_ref[...].reshape(count, rows // 2, 2, DH)
    out_ref[:, out_ref.shape[1] - rows // 2 :] = fresh


def place(packed, fresh):
    return call(
        place_kernel,
        jax.ShapeDtypeStruct(packed.shape, packed.dtype),
        [IN_VMEM] * 2,
        "place",
        input_output_aliases={0: 0},
    )(packed, fresh)


def attention_kernel(packed_ref, turn_ref, valid_ref, out_ref, *, span):
    f32, bf16 = jnp.float32, jnp.bfloat16
    sources = packed_ref.shape[0]
    pairs = span // 2
    sums = packed_ref[0, 2 * pairs :].reshape(-1, DH).astype(f32)
    for source in range(1, sources):
        sums = sums + packed_ref[source, 2 * pairs :].reshape(-1, DH).astype(f32)
    sums = sums.astype(bf16)
    plain = sums.astype(f32)
    swapped = pltpu.roll(plain, DH // 2, 1)
    turned = (plain * turn_ref[0:1] + swapped * turn_ref[1:2]).astype(bf16)
    query = turned[:GROUP]
    new_key = turned[GROUP : GROUP + 1]
    new_value = sums[GROUP + 1 : GROUP + 2]

    factor = DH ** (-0.5)
    keys = packed_ref[:, :pairs].reshape(-1, DH)
    values = packed_ref[:, pairs : 2 * pairs].reshape(-1, DH)
    scores = lax.dot_general(
        query, keys, (((1,), (1,)), ((), ())), preferred_element_type=f32
    ) * factor
    own = jnp.sum(query.astype(f32) * new_key.astype(f32), -1, keepdims=True) * factor
    valid = valid_ref[...] > 0
    top = jnp.maximum(jnp.max(jnp.where(valid, scores, LOWEST), -1, keepdims=True), own)
    weight = jnp.where(valid, jnp.exp(scores - top), 0.0)
    weight_own = jnp.exp(own - top)
    total = jnp.sum(weight, -1, keepdims=True) + weight_own
    mixed = jnp.dot(weight.astype(bf16), values, preferred_element_type=f32)
    mixed = mixed + weight_own.astype(bf16).astype(f32) * new_value.astype(f32)
    attention = (mixed / total).astype(bf16)

    for half, extra in enumerate((new_key, new_value)):
        first = half * HALF
        rows = jnp.concatenate([attention[first : first + HALF], extra, extra], 0)
        out_ref[:, half] = jnp.broadcast_to(rows[None], (out_ref.shape[0],) + rows.shape)


def attend(packed, turn, valid, span):
    return call(
        functools.partial(attention_kernel, span=span),
        jax.ShapeDtypeStruct((KVH, 2, HALF + 2, DH), jnp.bfloat16),
        [IN_VMEM] * 3,
        "attend",
    )(packed, turn, valid)


def finish_kernel(parts_ref, attended_ref, new_kv_ref):
    width = attended_ref.shape[1]
    sources = parts_ref.shape[0]
    sums = parts_ref[0, :, :width].astype(jnp.float32)
    for source in range(1, sources):
        sums = sums + parts_ref[source, :, :width].astype(jnp.float32)
    attended_ref[...] = sums.astype(attended_ref.dtype)
    for source in range(sources):
        column = (source % 2 * KVH + source // 2) * DH
        new_kv_ref[:, pl.ds(column, DH)] = parts_ref[source, :, width:]


def finish(parts, width):
    sources, seqs = parts.shape[:2]
    return call(
        finish_kernel,
        [
            jax.ShapeDtypeStruct((seqs, width), parts.dtype),
            jax.ShapeDtypeStruct((seqs, sources * DH), parts.dtype),
        ],
        [IN_VMEM],
        "finish",
    )(parts)


def per_device(
    hidden_in, q_weight, kv_weight, o_weight, cache_keys, cache_values, lengths, positions
):
    f32, bf16 = jnp.float32, jnp.bfloat16
    seqs, span = cache_keys.shape[:2]
    tp = lax.axis_size(TP)
    batch = hidden_in.shape[0]
    rows = 2 * span + GROUP + 2
    places = span * lax.axis_size(WIDE)

    packed, turn, valid = prepare(
        cache_keys, cache_values, frequencies(), lengths, positions, rows, places
    )
    q_part = jnp.dot(hidden_in, q_weight, preferred_element_type=f32).astype(bf16)
    kv_part = jnp.dot(hidden_in, kv_weight, preferred_element_type=f32).astype(bf16)
    partial = jnp.concatenate([q_part, kv_part], 1).reshape(tp, seqs, -1)
    partial = exchange(partial, TP)

    q_rows = partial[:, :, : HALF * DH].reshape(KVH, 2, seqs, HALF, DH)
    q_rows = q_rows.transpose(2, 0, 1, 3, 4).reshape(seqs, KVH, GROUP, DH)
    kv_rows = partial[:, :, HALF * DH :].reshape(2, KVH, seqs, DH).transpose(2, 1, 0, 3)
    fresh = jnp.concatenate([q_rows, kv_rows], 2)
    packed = place(packed, fresh.reshape(seqs * KVH, -1, DH))
    packed = exchange(packed, WIDE)
    heads = attend(packed, turn, valid, span)

    heads = exchange(heads.reshape((KVH * 2,) + heads.shape[2:]), ("z", "core"))
    middle = HALF * DH // 2
    mixed = heads[:, :HALF].reshape(KVH, 2, 2, middle)
    fresh = heads[:, HALF : HALF + 2].reshape(KVH, 2, 2, DH)
    piece = jnp.concatenate([mixed, fresh], 3)
    piece = jnp.broadcast_to(piece[:, None], (KVH, seqs) + piece.shape[1:])
    piece = exchange(piece.reshape((KVH * seqs,) + piece.shape[2:]), ("yh", "x", "yl"))
    flat = jnp.concatenate([piece[:, :, 0, :middle], piece[:, :, 1, :middle]], 2)
    product = jnp.dot(flat.reshape(batch, -1), o_weight, preferred_element_type=f32).astype(bf16)
    out = jnp.concatenate([product, piece[:, :, 0, middle:].reshape(batch, -1)], 1)
    out = out.reshape(KVH, seqs, 2, -1).transpose(0, 2, 1, 3).reshape(tp, seqs, -1)
    out = exchange(out, TP)
    return finish(out, o_weight.shape[1])


def solution(mesh):
    fine = Mesh(mesh.devices.reshape(SIZES), AXES)
    in_specs = (
        P(None, WIDE),
        P(WIDE, TP),
        P(WIDE, TP),
        P(TP, WIDE),
        P(TP, WIDE, None),
        P(TP, WIDE, None),
        P(TP),
        P(TP),
    )
    out_specs = (P(TP, WIDE), P(TP, None))
    return jax.shard_map(
        per_device, mesh=fine, in_specs=in_specs, out_specs=out_specs, check_vma=False
    )
```

```python
import functools

import jax
import jax.numpy as jnp
import numpy as np
from jax import lax
from jax.experimental import pallas as pl
from jax.experimental.pallas import tpu as pltpu
from jax.sharding import Mesh
from jax.sharding import PartitionSpec as P

NH = 128
KVH = 8
DH = 128
GROUP = NH // KVH
HALF = GROUP // 2

LOWEST = -1e30
LIMIT = 8 * 2**20

AXES = ("far", "near", "z", "yh", "x", "core")
SIZES = (2, 2, 8, 2, 4, 2)
WIDE = ("far", "near", "z")
TP = ("yh", "x", "core")


def exchange(array, axes):
    return lax.all_to_all(array, axes, split_axis=0, concat_axis=0, tiled=True)


def frequencies():
    half = DH // 2
    power = -(np.arange(half, dtype=np.float32) * np.float32(2.0) / np.float32(DH))
    freq = np.power(np.float64(500000.0), power.astype(np.float64)).astype(np.float32)
    return np.concatenate([freq, freq])[None]


def call(kernel, out_shape, in_specs, name, **options):
    return pl.pallas_call(
        kernel,
        out_shape=out_shape,
        in_specs=in_specs,
        out_specs=jax.tree.map(lambda _: pl.BlockSpec(memory_space=pltpu.VMEM), out_shape),
        compiler_params=pltpu.CompilerParams(vmem_limit_bytes=LIMIT),
        name=name,
        **options,
    )


IN_VMEM = pl.BlockSpec(memory_space=pltpu.VMEM)


def prepare_kernel(
    keys_ref, values_ref, freq_ref, lengths_ref, positions_ref, packed_ref, turn_ref, valid_ref
):
    seqs, span = keys_ref.shape[:2]
    pairs = span // 2
    for seq in range(seqs):
        for head in range(KVH):
            place = seq * KVH + head
            columns = pl.ds(head * DH, DH)
            packed_ref[place, :pairs] = keys_ref[seq, :, columns].reshape(pairs, 2, DH)
            packed_ref[place, pairs : 2 * pairs] = values_ref[seq, :, columns].reshape(pairs, 2, DH)
    lane = lax.broadcasted_iota(jnp.int32, lengths_ref.shape, 1)
    chosen = lane == lax.axis_index(("far", "near"))
    length = jnp.sum(jnp.where(chosen, lengths_ref[...], 0), axis=1, keepdims=True)
    position = jnp.sum(jnp.where(chosen, positions_ref[...], 0), axis=1, keepdims=True)
    valid = lax.broadcasted_iota(jnp.int32, valid_ref.shape, 1) < length
    valid_ref[...] = valid.astype(jnp.float32)
    angle = position.astype(jnp.float32) * freq_ref[...]
    sine = jnp.sin(angle)
    first_half = lax.broadcasted_iota(jnp.int32, sine.shape, 1) < DH // 2
    turn_ref[0:1] = jnp.cos(angle)
    turn_ref[1:2] = jnp.where(first_half, -sine, sine)


def prepare(cache_keys, cache_values, freq, lengths, positions, rows, places):
    seqs = cache_keys.shape[0]
    return call(
        prepare_kernel,
        [
            jax.ShapeDtypeStruct((seqs * KVH, rows // 2, 2, DH), cache_keys.dtype),
            jax.ShapeDtypeStruct((2, DH), jnp.float32),
            jax.ShapeDtypeStruct((1, places), jnp.float32),
        ],
        [IN_VMEM] * 5,
        "prepare",
    )(cache_keys, cache_values, freq, lengths[None], positions[None])


def place_kernel(packed_ref, fresh_ref, out_ref):
    del packed_ref
    count, rows = fresh_ref.shape[:2]
    pairs = rows // 2
    first = out_ref.shape[1] - rows
    fresh = fresh_ref[...]
    high = fresh.astype(out_ref.dtype)
    low = (fresh - high.astype(jnp.float32)).astype(out_ref.dtype)
    out_ref[:, first : first + pairs] = high.reshape(count, pairs, 2, DH)
    out_ref[:, first + pairs :] = low.reshape(count, pairs, 2, DH)


def place(packed, fresh):
    return call(
        place_kernel,
        jax.ShapeDtypeStruct(packed.shape, packed.dtype),
        [IN_VMEM] * 2,
        "place",
        input_output_aliases={0: 0},
    )(packed, fresh)


def attention_kernel(packed_ref, turn_ref, valid_ref, out_ref, *, span):
    f32, bf16 = jnp.float32, jnp.bfloat16
    sources = packed_ref.shape[0]
    pairs = span // 2
    split = (2 * pairs + packed_ref.shape[1]) // 2
    quarter = HALF // 2
    sums = []
    for near in range(2):
        total = 0.0
        for source in range(sources):
            if source // KVH % 2 == near:
                high = packed_ref[source, 2 * pairs : split].reshape(-1, DH).astype(f32)
                low = packed_ref[source, split:].reshape(-1, DH).astype(f32)
                total = total + (high + low)
        sums.append(total.astype(bf16).astype(f32))
    plain = jnp.concatenate(
        [
            sums[0][:quarter],
            sums[1][:quarter],
            sums[0][quarter:HALF],
            sums[1][quarter:HALF],
            sums[0][HALF:],
            sums[0][HALF:],
            sums[0][HALF:],
            sums[0][HALF:],
        ],
        0,
    )
    swapped = pltpu.roll(plain, DH // 2, 1)
    turned = (plain * turn_ref[0:1] + swapped * turn_ref[1:2]).astype(bf16)
    query = turned[:GROUP]
    new_key = turned[GROUP : GROUP + 1]
    new_value = plain[GROUP + 1 : GROUP + 2].astype(bf16)

    factor = DH ** (-0.5)
    keys = packed_ref[:, :pairs].reshape(-1, DH)
    values = packed_ref[:, pairs : 2 * pairs].reshape(-1, DH)
    scores = lax.dot_general(
        query, keys, (((1,), (1,)), ((), ())), preferred_element_type=f32
    ) * factor
    own = jnp.sum(query.astype(f32) * new_key.astype(f32), -1, keepdims=True) * factor
    valid = valid_ref[...] > 0
    top = jnp.maximum(jnp.max(jnp.where(valid, scores, LOWEST), -1, keepdims=True), own)
    weight = jnp.where(valid, jnp.exp(scores - top), 0.0)
    weight_own = jnp.exp(own - top)
    total = jnp.sum(weight, -1, keepdims=True) + weight_own
    mixed = jnp.dot(weight.astype(bf16), values, preferred_element_type=f32)
    mixed = mixed + weight_own.astype(bf16).astype(f32) * new_value.astype(f32)
    attention = (mixed / total).astype(bf16)

    for half, extra in enumerate((new_key, new_value)):
        first = half * HALF
        rows = jnp.concatenate([attention[first : first + HALF], extra, extra], 0)
        rows = rows.reshape(HALF // 2 + 1, 2, DH)
        out_ref[:, half] = jnp.broadcast_to(rows[None], (out_ref.shape[0],) + rows.shape)


def attend(packed, turn, valid, span):
    return call(
        functools.partial(attention_kernel, span=span),
        jax.ShapeDtypeStruct((KVH, 2, HALF // 2 + 1, 2, DH), jnp.bfloat16),
        [IN_VMEM] * 3,
        "attend",
    )(packed, turn, valid)


def finish_kernel(parts_ref, attended_ref, new_kv_ref):
    width = attended_ref.shape[1]
    sources = parts_ref.shape[0]
    sums = parts_ref[0, :, :width].astype(jnp.float32)
    for source in range(1, sources):
        sums = sums + parts_ref[source, :, :width].astype(jnp.float32)
    attended_ref[...] = sums.astype(attended_ref.dtype)
    for source in range(sources):
        column = (source % 2 * KVH + source // 2) * DH
        new_kv_ref[:, pl.ds(column, DH)] = parts_ref[source, :, width:]


def finish(parts, width):
    sources, seqs = parts.shape[:2]
    return call(
        finish_kernel,
        [
            jax.ShapeDtypeStruct((seqs, width), parts.dtype),
            jax.ShapeDtypeStruct((seqs, sources * DH), parts.dtype),
        ],
        [IN_VMEM],
        "finish",
    )(parts)


def per_device(
    hidden_in, q_weight, kv_weight, o_weight, cache_keys, cache_values, lengths, positions
):
    f32, bf16 = jnp.float32, jnp.bfloat16
    seqs, span = cache_keys.shape[:2]
    tp = lax.axis_size(TP)
    batch = hidden_in.shape[0]
    rows = 2 * span + 2 * (HALF + 2)
    places = span * lax.axis_size(WIDE)

    packed, turn, valid = prepare(
        cache_keys, cache_values, frequencies(), lengths, positions, rows, places
    )
    q_part = jnp.dot(hidden_in, q_weight, preferred_element_type=f32)
    kv_part = jnp.dot(hidden_in, kv_weight, preferred_element_type=f32)
    middle = HALF * DH // 2
    partial = jnp.stack(
        [
            jnp.concatenate([q_part[:, :middle], kv_part], 1),
            jnp.concatenate([q_part[:, middle:], jnp.zeros_like(kv_part)], 1),
        ]
    )
    partial = exchange(partial.reshape(2 * tp, seqs, -1), ("near",) + TP)
    partial = jnp.sum(partial.reshape(2, tp, seqs, -1), 0)

    q_rows = partial[:, :, :middle].reshape(KVH, 2, seqs, HALF // 2, DH)
    q_rows = q_rows.transpose(2, 0, 1, 3, 4).reshape(seqs, KVH, HALF, DH)
    kv_rows = partial[:, :, middle:].reshape(2, KVH, seqs, DH).transpose(2, 1, 0, 3)
    fresh = jnp.concatenate([q_rows, kv_rows], 2)
    packed = place(packed, fresh.reshape(seqs * KVH, -1, DH))
    packed = exchange(packed, WIDE)
    heads = attend(packed, turn, valid, span)

    heads = exchange(heads.reshape((KVH * 2,) + heads.shape[2:]), ("z", "core"))
    piece = heads.reshape((KVH, 1, -1) + heads.shape[2:])
    piece = jnp.broadcast_to(piece, (KVH, seqs) + piece.shape[2:])
    piece = exchange(piece.reshape((KVH * seqs,) + piece.shape[2:]), ("yh", "x", "far", "near"))
    piece = piece.reshape(batch, HALF + 2, DH)
    flat = piece[:, :HALF].reshape(batch, -1)
    product = jnp.dot(flat, o_weight, preferred_element_type=f32).astype(bf16)
    out = jnp.concatenate([product, piece[:, HALF]], 1)
    out = out.reshape(KVH, seqs, 2, -1).transpose(0, 2, 1, 3).reshape(tp, seqs, -1)
    out = exchange(out, TP)
    return finish(out, o_weight.shape[1])


def solution(mesh):
    fine = Mesh(mesh.devices.reshape(SIZES), AXES)
    in_specs = (
        P(None, WIDE),
        P(WIDE, TP),
        P(WIDE, TP),
        P(TP, WIDE),
        P(TP, WIDE, None),
        P(TP, WIDE, None),
        P(TP),
        P(TP),
    )
    out_specs = (P(TP, WIDE), P(TP, None))
    return jax.shard_map(
        per_device, mesh=fine, in_specs=in_specs, out_specs=out_specs, check_vma=False
    )
```
